32 devices in a mesh: groups: 2 (over y), dp: 8 (over z, x), tensor: 2 (over core).
Axes of the slice: x: 2, y: 2, z: 4, core: 2. Of those that a mesh axis runs over, the one named last changes fastest.
Arguments:
- inputs: bfloat16 [2048, 8192], P(('groups', 'dp'), 'tensor'), parts along dimension 0, may hold values from -6 to 6
- output_gradient: bfloat16 [2048, 4096], P(('groups', 'dp')), parts along dimension 0, may hold values from -6 to 6
- frozen_output: bfloat16 [2048, 4096], P(('groups', 'dp')), parts along dimension 0, may hold values from -6 to 6
- tenant_of_tile: int32 [32], P(('groups', 'dp')), parts along dimension 0, may hold values from 0 to 7, as said below
- frozen_weight: bfloat16 [4096, 8192], P('dp', 'tensor'), may hold values from -1 to 1
- adapter_down: bfloat16 [8, 16, 8192], P(None, None, 'tensor'), may hold values from -2 to 2
- adapter_up: bfloat16 [8, 4096, 16], P(None, 'dp'), may hold values from -1.5 to 1.5
- magnitude: float32 [8, 4096], P(None, 'dp'), may hold values from 0.5 to 2
Outputs:
- grad_up: float32 [16, 4096, 16], P('groups', ('dp', 'tensor')), parts along dimension 0
- grad_mag: float32 [16, 4096], P('groups', ('dp', 'tensor')), parts along dimension 0
- grad_down: float32 [256, 8192], P(('groups', 'dp'), 'tensor'), parts along dimension 0
The draws below stay inside these ranges and needn't reach their ends.
There are 2 independent parts, one for each index of `groups`. The reference program is written for one: setup_inputs(seed, part) draws one part's arguments, and reference() takes and returns one part's arrays. A program takes and returns all parts, laid end to end along the dimension named above; an argument that names none is the same for every part. Nothing has to cross between parts.
Inputs may be any that keep to these rules, and one draw needn't show every extreme that they name: `tenant_of_tile`: within the 2 tiles of each index of dp the tenants do not decrease; every tenant owns at least one tile.
All inputs are finite; a program needn't handle non-finite values.
Results may differ from the reference program's by a relative error of at most 0.0037.
The reference program's roundings to bfloat16 on the way (of `rank_act`, `scaled_grad` and `rank_grad`) count: a program that leaves them out, or rounds other values in their place, can miss the bound.
Values may be sent and summed in bfloat16 or wider, within the bound.
A program may use at most 64 MiB of HBM per device.

```python
import math
import jax
import jax.numpy as jnp
from jax import lax

INPUT_FEATURES = 8192
OUTPUT_FEATURES = 4096
ADAPTER_RANK = 16
TENANT_COUNT = 8
TILE = 64
TOK_DEV = 128
TOKENS = 1024
TILES = 16


def shared_direction(key):
    raw = jax.random.normal(key, (INPUT_FEATURES,), jnp.float32)
    return jnp.clip(raw, -4.0, 4.0) / math.sqrt(INPUT_FEATURES)


def draw_tenant_of_tile(key, part):
    key = jax.random.fold_in(key, 7)
    key_tiles, key_spots = jax.random.split(key)
    drawn = jax.random.randint(key_tiles, (TILES,), 0, TENANT_COUNT).astype(jnp.int32)
    spots = jax.random.permutation(key_spots, TILES)[:TENANT_COUNT]
    drawn = drawn.at[spots].set(jnp.arange(TENANT_COUNT, dtype=jnp.int32))
    per_device = TOK_DEV // TILE
    blocks = jnp.sort(drawn.reshape(TILES // per_device, per_device), axis=1)
    return blocks.reshape(TILES).astype(jnp.int32)


def draw_frozen_weight(key, part):
    direction = shared_direction(key)
    key = jax.random.fold_in(key, 11)
    key_coef, key_noise = jax.random.split(key)
    coef = jax.random.uniform(key_coef, (OUTPUT_FEATURES, 1), jnp.float32, -1.0, 1.0)
    noise = jnp.clip(jax.random.normal(key_noise, (OUTPUT_FEATURES, INPUT_FEATURES), jnp.float32), -4.0, 4.0)
    values = coef * direction[None, :] + noise / math.sqrt(INPUT_FEATURES)
    return values.astype(jnp.bfloat16)


def draw_adapter_down(key, part):
    direction = shared_direction(key)
    key = jax.random.fold_in(key, 13)
    key_along, key_common, key_noise = jax.random.split(key, 3)
    along = jax.random.uniform(key_along, (TENANT_COUNT, ADAPTER_RANK, 1), jnp.float32, -1.0, 1.0)
    common = jnp.clip(jax.random.normal(key_common, (TENANT_COUNT, 1, INPUT_FEATURES), jnp.float32), -4.0, 4.0)
    noise = jnp.clip(jax.random.normal(key_noise, (TENANT_COUNT, ADAPTER_RANK, INPUT_FEATURES), jnp.float32), -4.0, 4.0)
    values = along * direction[None, None, :] + (0.5 * common + noise) / math.sqrt(INPUT_FEATURES)
    return values.astype(jnp.bfloat16)


def shard_levels(stream_key, extent, shards, least, top_value):
    level, own = 1.0, jax.random.fold_in(stream_key, 6)
    for dim, parts in shards:
        steps = jnp.exp(jax.random.uniform(jax.random.fold_in(own, dim), (parts,), jnp.float32, least / len(shards), top_value / len(shards)))
        level = level * jnp.repeat(steps, extent[dim] // parts).reshape([-1 if axis == dim else 1 for axis in range(len(extent))])
    return level


def gaussian(rng, dims, scale, most, pieces=(), kind=jnp.bfloat16):
    gain = shard_levels(rng, dims, pieces, -0.22, 0.18) if pieces else 1.0
    entries = jax.random.normal(rng, dims, jnp.float32) * scale * gain
    return jnp.minimum(jnp.maximum(entries, -most), most).astype(kind)


def setup_inputs(seed: int = 0, part: int = 0) -> dict:
    splits = jax.random.split(jax.random.key(seed), 9)
    part_splits = jax.random.split(jax.random.fold_in(splits[8], part), 9)
    inputs = gaussian(part_splits[0], (TOKENS, INPUT_FEATURES), 1.0, 6.0, ((0, 8), (1, 2)))
    output_gradient = gaussian(part_splits[1], (TOKENS, OUTPUT_FEATURES), 1.0, 6.0, ((0, 8),))
    frozen_output = gaussian(part_splits[2], (TOKENS, OUTPUT_FEATURES), 1.0, 6.0, ((0, 8),))
    tenant_of_tile = draw_tenant_of_tile(jax.random.fold_in(jax.random.fold_in(splits[8], part), 71), part)
    frozen_weight = draw_frozen_weight(jax.random.fold_in(splits[8], 71), part)
    adapter_down = draw_adapter_down(jax.random.fold_in(splits[8], 71), part)
    adapter_up = gaussian(splits[6], (TENANT_COUNT, OUTPUT_FEATURES, ADAPTER_RANK), 0.25, 1.5, ((1, 8),))
    magnitude = jnp.clip(jnp.exp(math.log(2.0) - 1.3862944 * jax.random.uniform(splits[7], (TENANT_COUNT, OUTPUT_FEATURES), jnp.float32) ** shard_levels(splits[7], (TENANT_COUNT, OUTPUT_FEATURES), ((1, 8),), -0.2, 0.2)), 0.5, 2.0)
    return dict(inputs=inputs, output_gradient=output_gradient, frozen_output=frozen_output, tenant_of_tile=tenant_of_tile, frozen_weight=frozen_weight, adapter_down=adapter_down, adapter_up=adapter_up, magnitude=magnitude)


def reference(inputs, output_gradient, frozen_output, tenant_of_tile, frozen_weight, adapter_down, adapter_up, magnitude):
    hi = lax.Precision.HIGHEST
    base_f = frozen_weight.astype(jnp.float32)

    def squared_rows(tenant_pair):
        up_one, down_one = tenant_pair
        merged = base_f + jnp.dot(up_one, down_one, preferred_element_type=jnp.float32)
        return lax.optimization_barrier(jnp.sum(merged * merged, axis=1))
    norm_values = jnp.sqrt(lax.map(squared_rows, (adapter_up, adapter_down)))
    scales = magnitude / norm_values
    ten_ids = jnp.repeat(tenant_of_tile, TILE)
    member = ten_ids[:, None] == jnp.arange(TENANT_COUNT, dtype=jnp.int32)[None, :]
    member_f = member.astype(jnp.float32)
    member_b = member.astype(jnp.bfloat16)
    down_flattened = adapter_down.reshape(TENANT_COUNT * ADAPTER_RANK, INPUT_FEATURES)
    projected = lax.dot_general(inputs, down_flattened, (((1,), (1,)), ((), ())), preferred_element_type=jnp.float32)
    rank_act = lax.optimization_barrier(jnp.sum(projected.reshape(TOKENS, TENANT_COUNT, ADAPTER_RANK) * member_f[:, :, None], axis=1)).astype(jnp.bfloat16)
    wide_rank = (member_b[:, :, None] * rank_act[:, None, :]).reshape(TOKENS, TENANT_COUNT * ADAPTER_RANK)
    flattened_up = jnp.transpose(adapter_up, (0, 2, 1)).reshape(TENANT_COUNT * ADAPTER_RANK, OUTPUT_FEATURES)
    mixed_out = frozen_output.astype(jnp.float32) + jnp.dot(wide_rank, flattened_up, preferred_element_type=jnp.float32)
    grad_f = output_gradient.astype(jnp.float32)
    grad_mag = jnp.dot(member_f.T, grad_f * mixed_out, precision=hi) / norm_values
    tok_scale = jnp.dot(member_f, scales, precision=hi)
    scaled_grad = (grad_f * tok_scale).astype(jnp.bfloat16)
    up_sum = lax.dot_general(wide_rank, scaled_grad, (((0,), (0,)), ((), ())), preferred_element_type=jnp.float32)
    grad_up = jnp.transpose(up_sum.reshape(TENANT_COUNT, ADAPTER_RANK, OUTPUT_FEATURES), (0, 2, 1))
    back_full = lax.dot_general(scaled_grad, flattened_up, (((1,), (1,)), ((), ())), preferred_element_type=jnp.float32)
    rank_grad = lax.optimization_barrier(jnp.sum(back_full.reshape(TOKENS, TENANT_COUNT, ADAPTER_RANK) * member_f[:, :, None], axis=1)).astype(jnp.bfloat16)
    wide_back = (member_b[:, :, None] * rank_grad[:, None, :]).reshape(TOKENS, TENANT_COUNT * ADAPTER_RANK)
    grad_down = lax.dot_general(wide_back, inputs, (((0,), (0,)), ((), ())), preferred_element_type=jnp.float32)
    return (grad_up, grad_mag, grad_down)
```

```python
import functools

import jax
import jax.numpy as jnp
from jax import lax
from jax.experimental import pallas as pl
from jax.experimental.pallas import tpu as pltpu
from jax.sharding import PartitionSpec as P


def plain(
    inputs,
    output_gradient,
    frozen_output,
    tenant_of_tile,
    frozen_weight,
    adapter_down,
    adapter_up,
    magnitude,
):
    hi = lax.Precision.HIGHEST
    tenant_list, rank_dimension, input_local = adapter_down.shape
    own_rows = frozen_weight.shape[0]
    token_rows = inputs.shape[0]
    tile_count = tenant_of_tile.shape[0]
    tile_len = token_rows // tile_count
    tensor_count = lax.axis_size("tensor")
    data_count = lax.axis_size("dp")
    row_halves_split = own_rows // tensor_count
    span_cols = data_count * row_halves_split
    shifted_values = jnp.einsum(
        "sxh,shj->sxj", adapter_up, adapter_down, preferred_element_type=jnp.float32
    )
    merged = frozen_weight.astype(jnp.float32)[None] + shifted_values
    partial_sq = jnp.sum(merged * merged, axis=2)
    tile_onehot = (
        tenant_of_tile[:, None] == jnp.arange(tenant_list, dtype=jnp.int32)[None, :]
    ).astype(jnp.float32)
    row_tenant = jnp.repeat(jnp.arange(tenant_list, dtype=jnp.int32), rank_dimension)
    row_rank = jnp.tile(jnp.arange(rank_dimension, dtype=jnp.int32), tenant_list)
    col_tenant = jnp.repeat(tenant_of_tile, rank_dimension)
    col_rank = jnp.tile(jnp.arange(rank_dimension, dtype=jnp.int32), tile_count)
    placement = (
        (row_tenant[:, None] == col_tenant[None, :]) & (row_rank[:, None] == col_rank[None, :])
    ).astype(jnp.float32)
    tile_inputs = inputs.reshape(tile_count, tile_len, input_local)
    selected_down = jnp.take(adapter_down, tenant_of_tile, axis=0)
    rank_part = jnp.einsum(
        "tsi,tri->tsr", tile_inputs, selected_down, preferred_element_type=jnp.float32
    )
    norm_sq = lax.psum(partial_sq, "tensor")
    rank_sum = lax.psum(rank_part, "tensor")
    norm_values = jnp.sqrt(norm_sq)
    tile_position = lax.axis_index("tensor") * row_halves_split
    scale_own = lax.dynamic_slice_in_dim(
        magnitude / norm_values, tile_position, row_halves_split, 1
    )
    norm_own = lax.dynamic_slice_in_dim(norm_values, tile_position, row_halves_split, 1)
    owned_up_rows = lax.dynamic_slice_in_dim(adapter_up, tile_position, row_halves_split, 1)
    scales = lax.all_gather(scale_own, "dp", axis=1, tiled=True)
    up_cols = lax.all_gather(owned_up_rows, "dp", axis=1, tiled=True)

    def select_cols(full):
        shaped = full.reshape(token_rows, data_count, tensor_count, row_halves_split)
        picked = lax.dynamic_index_in_dim(shaped, lax.axis_index("tensor"), 2, keepdims=False)
        return picked.reshape(tile_count, tile_len, span_cols)

    grad_cols = select_cols(output_gradient)
    base_cols = select_cols(frozen_output)
    rank_low = rank_sum.astype(jnp.bfloat16)
    up_sel = jnp.take(up_cols, tenant_of_tile, axis=0)
    scale_sel = jnp.take(scales, tenant_of_tile, axis=0)
    mixed_out = base_cols.astype(jnp.float32) + jnp.einsum(
        "tsr,tor->tso", rank_low, up_sel, preferred_element_type=jnp.float32
    )
    grad_f = grad_cols.astype(jnp.float32)
    tile_mag = jnp.sum(grad_f * mixed_out, axis=1)
    mag_part = jnp.dot(tile_onehot.T, tile_mag, precision=hi)
    scaled_grad = (grad_f * scale_sel[:, None, :]).astype(jnp.bfloat16)
    up_tile = jnp.einsum("tsr,tso->tro", rank_low, scaled_grad, preferred_element_type=jnp.float32)
    up_part = jnp.dot(
        placement, up_tile.reshape(tile_count * rank_dimension, span_cols), precision=hi
    )
    back_part = jnp.einsum("tso,tor->tsr", scaled_grad, up_sel, preferred_element_type=jnp.float32)
    back_sum = lax.psum(back_part, "tensor")
    back_low = back_sum.astype(jnp.bfloat16)
    down_tile = jnp.einsum(
        "tsr,tsi->tri", back_low, tile_inputs, preferred_element_type=jnp.float32
    ).reshape(tile_count * rank_dimension, input_local)
    up_sum = lax.psum_scatter(up_part, "dp", scatter_dimension=1, tiled=True)
    mag_sum = lax.psum_scatter(mag_part, "dp", scatter_dimension=1, tiled=True)
    grad_mag = mag_sum / norm_own
    grad_up = jnp.transpose(
        up_sum.reshape(tenant_list, rank_dimension, row_halves_split), (0, 2, 1)
    )
    down_part = jnp.dot(placement, down_tile, precision=hi)
    grad_down = lax.psum_scatter(down_part, "dp", scatter_dimension=0, tiled=True)
    return (grad_up, grad_mag, grad_down)


F32 = jnp.float32
BF16 = jnp.bfloat16
NT = (((1,), (1,)), ((), ()))


def iota(shape, dim):
    return lax.broadcasted_iota(jnp.int32, shape, dim)


def exchange_kernel(
    N, T, K, R,
    ten_ref, x_ref, g_ref, f_ref, down_ref, up_ref, mag_ref, sq_ref,
    up_out, mag_out, down_out,
    g_buf, aux_send, aux_buf, sq_buf, rp_send, rp_buf, ra_buf, up_acc, z_acc, fg_acc,
    back_send, back_buf, tile_send, tile_buf, part_send, part_buf,
    g_ss, g_rs, aux_ss, aux_rs, pair_ss, pair_rs, ra_ss, ra_rs,
    back_ss, back_rs, tile_ss, tile_rs, part_ss, part_rs,
):
    me = lax.axis_index("dp")
    core = lax.axis_index("tensor")
    other = 1 - core
    tok = x_ref.shape[0]
    half = tok // 2
    width = x_ref.shape[1] // N
    C = up_ref.shape[1]
    KR = K * R

    def copy(src, dst, ss, rs, dp, tensor):
        return pltpu.make_async_remote_copy(
            src_ref=src, dst_ref=dst, send_sem=ss, recv_sem=rs,
            device_id={"dp": dp, "tensor": tensor}, device_id_type=pl.DeviceIdType.MESH,
        )

    def peer(off):
        return lax.rem(me + off, N)

    barrier = pltpu.get_barrier_semaphore()
    for off in range(N):
        for t in ((other,) if off == 0 else (core, other)):
            pl.semaphore_signal(
                barrier, inc=1, device_id={"dp": peer(off), "tensor": t},
                device_id_type=pl.DeviceIdType.MESH,
            )
    pl.semaphore_wait(barrier, 2 * N - 1)

    def cols(d):
        return pl.ds(pl.multiple_of((d * T + core) * C, C), C)

    def span(d):
        return pl.ds(pl.multiple_of(d * width, width), width)

    def g_copy(d):
        return copy(g_ref.at[:, cols(d)], g_buf.at[me], g_ss.at[d], g_rs.at[me], d, core)

    def aux_copy(d):
        return copy(aux_send.at[d], aux_buf.at[me], aux_ss.at[d], aux_rs.at[me], d, core)

    sq_copy = copy(
        sq_ref.at[:, pl.ds(pl.multiple_of(other * C, C), C)], sq_buf,
        pair_ss.at[0], pair_rs.at[0], me, other,
    )
    sq_copy.start()

    def start_g(off, _):
        g_copy(peer(off)).start()
        return 0
    lax.fori_loop(1, N, start_g, 0)

    ten0 = ten_ref[0]
    ten1 = ten_ref[1]
    lane_tok = iota((1, tok), 1)
    own_ten = jnp.where(lane_tok < half, ten0, ten1)
    own_mask = (iota((KR, tok), 0) // R) == own_ten

    proj = lax.dot_general(down_ref[...], x_ref[...], NT, preferred_element_type=F32)
    rp_send[...] = jnp.sum(jnp.where(own_mask, proj, 0.0).reshape(K, R, tok), axis=0)
    rp_copy = copy(rp_send, rp_buf, pair_ss.at[1], pair_rs.at[1], me, other)
    rp_copy.start()

    lane = iota((1, C), 1)
    rows = iota((8, C), 0)
    ids0 = jnp.full((1, C), ten0, jnp.int32)
    ids1 = jnp.full((1, C), ten1, jnp.int32)
    tok_ids = jnp.where(lax.rem(lane, tok) < half, ten0, ten1)
    slot_ids = jnp.where(lane // (2 * R) == me, jnp.where(lax.rem(lane, 2 * R) < R, ten0, ten1), 0)
    ids = jnp.where(rows == 2, ids0, jnp.where(rows == 3, ids1, jnp.where(rows == 4, tok_ids, slot_ids)))
    ids = jnp.where((rows >= 2) & (rows <= 5), ids, 0).astype(F32)

    def make_aux(off, _):
        d = peer(off)
        prod = g_ref[:, cols(d)].astype(F32) * f_ref[:, cols(d)].astype(F32)
        s0 = jnp.sum(prod[:half], axis=0, keepdims=True)
        s1 = jnp.sum(prod[half:], axis=0, keepdims=True)
        aux_send[d] = jnp.where(rows == 0, s0, jnp.where(rows == 1, s1, ids))
        return 0

    def start_aux(off, _):
        make_aux(off, 0)
        aux_copy(peer(off)).start()
        return 0
    lax.fori_loop(1, N, start_aux, 0)
    make_aux(0, 0)
    aux_buf[me] = aux_send[me]
    g_buf[me] = g_ref[:, cols(me)]

    rp_copy.wait_recv()
    a = rp_send[...]
    b = rp_buf[...]
    ra_buf[me] = (a + b).astype(BF16)

    def ra_copy(d):
        return copy(ra_buf.at[me], ra_buf.at[me], ra_ss.at[d], ra_rs.at[me], d, core)

    def start_ra(off, _):
        ra_copy(peer(off)).start()
        return 0
    lax.fori_loop(1, N, start_ra, 0)

    sq_copy.wait_recv()
    norm = jnp.sqrt(sq_ref[:, pl.ds(pl.multiple_of(core * C, C), C)] + sq_buf[...])
    scale = mag_ref[...] / norm
    up = up_ref[...]

    up_acc[...] = jnp.zeros_like(up_acc)
    z_acc[...] = jnp.zeros_like(z_acc)
    fg_acc[...] = jnp.zeros_like(fg_acc)

    def owner_block(s):
        aux = aux_buf[s]
        fg = fg_acc[...]
        sel0 = jnp.zeros((1, C), F32)
        sel1 = jnp.zeros((1, C), F32)
        krow = iota((K, C), 0).astype(F32)
        hit0 = krow == aux[2:3]
        hit1 = krow == aux[3:4]
        fg_acc[...] = fg + jnp.where(hit0, aux[0:1], 0.0) + jnp.where(hit1, aux[1:2], 0.0)
        sel0 = jnp.sum(jnp.where(hit0, scale, 0.0), axis=0, keepdims=True)
        sel1 = jnp.sum(jnp.where(hit1, scale, 0.0), axis=0, keepdims=True)
        g = g_buf[s]
        gf = g.astype(F32)
        scaled = (gf * jnp.where(iota((tok, C), 0) < half, sel0, sel1)).astype(BF16)
        mask = (iota((KR, tok), 0) // R).astype(F32) == aux[4:5, :tok]
        ra = ra_buf[s].astype(F32)
        wide = jnp.where(mask, jnp.concatenate([ra] * K, axis=0), 0.0).astype(BF16)
        up_acc[...] += jnp.dot(wide, scaled, preferred_element_type=F32)
        z_acc[...] += jnp.dot(wide, g, preferred_element_type=F32)
        back = lax.dot_general(up, scaled, NT, preferred_element_type=F32)
        return jnp.sum(jnp.where(mask, back, 0.0).reshape(K, R, tok), axis=0)

    mine = me * T + core

    def back_copy(s, t):
        return copy(
            back_send.at[s], back_buf.at[mine], back_ss.at[s * T + t], back_rs.at[mine], s, t
        )

    own_back = owner_block(me)
    back_send[me] = own_back
    back_copy(me, other).start()
    back_buf[mine] = own_back

    def remote_block(off, _):
        s = peer(off)
        copy(aux_send.at[s], aux_buf.at[s], aux_ss.at[s], aux_rs.at[s], s, core).wait_recv()
        copy(ra_buf.at[s], ra_buf.at[s], ra_ss.at[s], ra_rs.at[s], s, core).wait_recv()
        copy(g_buf.at[s], g_buf.at[s], g_ss.at[s], g_rs.at[s], s, core).wait_recv()
        back_send[s] = owner_block(s)
        back_copy(s, core).start()
        back_copy(s, other).start()
        return 0
    lax.fori_loop(1, N, remote_block, 0)

    up_sum = up_acc[...]
    up_out[...] = up_sum
    mixed = jnp.sum((up.astype(F32) * z_acc[...]).reshape(K, R, C), axis=1)
    mag_out[...] = (fg_acc[...] + mixed) / norm

    def wait_back(s, t):
        i = s * T + t
        copy(back_send.at[s], back_buf.at[i], back_ss.at[i], back_rs.at[i], s, t).wait_recv()

    def wait_backs(off, _):
        wait_back(peer(off), core)
        wait_back(peer(off), other)
        return 0
    wait_back(me, other)
    lax.fori_loop(1, N, wait_backs, 0)
    rank_grad = jnp.sum(back_buf[...], axis=0).astype(BF16).astype(F32)
    two = jnp.concatenate([rank_grad, rank_grad], axis=0)
    lhs = jnp.where((iota((2 * R, tok), 0) // R) == (iota((2 * R, tok), 1) // half), two, 0.0).astype(BF16)

    def tile_copy(d):
        return copy(tile_send.at[d], tile_buf.at[me], tile_ss.at[d], tile_rs.at[me], d, core)

    def start_tile(off, _):
        d = peer(off)
        tile_send[d] = jnp.dot(lhs, x_ref[:, span(d)], preferred_element_type=F32).astype(BF16)
        tile_copy(d).start()
        return 0
    lax.fori_loop(1, N, start_tile, 0)
    tile_buf[me] = jnp.dot(lhs, x_ref[:, span(me)], preferred_element_type=F32).astype(BF16)

    slot_ten = jnp.sum(aux_buf[:, 5, :], axis=0, keepdims=True)
    prow = iota((KR, C), 0)
    place = ((prow // R).astype(F32) == slot_ten) & (lax.rem(prow, R) == lax.rem(iota((KR, C), 1), R))
    place = jnp.where(place, 1.0, 0.0).astype(BF16)

    def wait_tile(off, _):
        s = peer(off)
        copy(tile_send.at[s], tile_buf.at[s], tile_ss.at[s], tile_rs.at[s], s, core).wait_recv()
        return 0
    lax.fori_loop(1, N, wait_tile, 0)
    part = jnp.dot(place, tile_buf[...].reshape(N * 2 * R, width), preferred_element_type=F32)
    part_send[...] = part.astype(BF16).reshape(N, R, width)

    def part_copy(d):
        return copy(part_send.at[d], part_buf.at[me], part_ss.at[d], part_rs.at[me], d, core)

    def start_part(off, _):
        part_copy(peer(off)).start()
        return 0
    lax.fori_loop(1, N, start_part, 0)
    part_buf[me] = part_send[me]

    def wait_sends(off, _):
        d = peer(off)
        g_copy(d).wait_send()
        aux_copy(d).wait_send()
        ra_copy(d).wait_send()
        back_copy(d, core).wait_send()
        back_copy(d, other).wait_send()
        tile_copy(d).wait_send()
        return 0
    sq_copy.wait_send()
    rp_copy.wait_send()
    back_copy(me, other).wait_send()
    lax.fori_loop(1, N, wait_sends, 0)

    down_out[:, span(me)] = part_buf[me].astype(F32)

    def finish(off, _):
        s = peer(off)
        copy(part_send.at[s], part_buf.at[s], part_ss.at[s], part_rs.at[s], s, core).wait_recv()
        down_out[:, span(s)] = part_buf[s].astype(F32)
        part_copy(s).wait_send()
        return 0
    lax.fori_loop(1, N, finish, 0)


def exchange(ten, x, g, f, down, up, mag, sq, N, T, K, R):
    tok, I = x.shape
    C = up.shape[1]
    width = I // N
    vm = pltpu.VMEM
    dma = pltpu.SemaphoreType.DMA
    spec = pl.BlockSpec(memory_space=pltpu.VMEM)
    return pl.pallas_call(
        functools.partial(exchange_kernel, N, T, K, R),
        out_shape=(
            jax.ShapeDtypeStruct((K * R, C), F32),
            jax.ShapeDtypeStruct((K, C), F32),
            jax.ShapeDtypeStruct((R, I), F32),
        ),
        in_specs=[pl.BlockSpec(memory_space=pltpu.SMEM)] + [spec] * 7,
        out_specs=(spec, spec, spec),
        scratch_shapes=[
            vm((N, tok, C), BF16), vm((N, 8, C), F32), vm((N, 8, C), F32), vm((K, C), F32),
            vm((R, tok), F32), vm((R, tok), F32), vm((N, R, tok), BF16),
            vm((K * R, C), F32), vm((K * R, C), F32), vm((K, C), F32),
            vm((N, R, tok), F32), vm((N * T, R, tok), F32),
            vm((N, 2 * R, width), BF16), vm((N, 2 * R, width), BF16),
            vm((N, R, width), BF16), vm((N, R, width), BF16),
            dma((N,)), dma((N,)), dma((N,)), dma((N,)), dma((2,)), dma((2,)),
            dma((N,)), dma((N,)), dma((N * T,)), dma((N * T,)),
            dma((N,)), dma((N,)), dma((N,)), dma((N,)),
        ],
        compiler_params=pltpu.CompilerParams(
            collective_id=0, has_side_effects=True, vmem_limit_bytes=40 * 1024 * 1024
        ),
    )(ten, x, g, f, down, up, mag, sq)


def partial_norms(weight, down, up):
    shifted = jnp.einsum("sxh,shj->sxj", up, down, preferred_element_type=F32)
    merged = weight.astype(F32)[None] + shifted
    return jnp.sum(merged * merged, axis=2)


def local(
    inputs,
    output_gradient,
    frozen_output,
    tenant_of_tile,
    frozen_weight,
    adapter_down,
    adapter_up,
    magnitude,
):
    K, R, I = adapter_down.shape
    N = lax.axis_size("dp")
    T = lax.axis_size("tensor")
    own = frozen_weight.shape[0]
    C = own // T
    if not (
        N == K and T == 2 and R == 16 and K == 8 and C == N * 2 * R
        and inputs.shape[0] == 128 and tenant_of_tile.shape[0] == 2 and I % (128 * N) == 0
    ):
        return plain(
            inputs, output_gradient, frozen_output, tenant_of_tile,
            frozen_weight, adapter_down, adapter_up, magnitude,
        )
    sq = partial_norms(frozen_weight, adapter_down, adapter_up)
    at = lax.axis_index("tensor") * C
    up = jnp.transpose(lax.dynamic_slice_in_dim(adapter_up, at, C, 1), (0, 2, 1)).reshape(K * R, C)
    mag = lax.dynamic_slice_in_dim(magnitude, at, C, 1)
    up_sum, grad_mag, grad_down = exchange(
        tenant_of_tile, inputs, output_gradient, frozen_output,
        adapter_down.reshape(K * R, I), up, mag, sq, N, T, K, R,
    )
    grad_up = jnp.transpose(up_sum.reshape(K, R, C), (0, 2, 1))
    return (grad_up, grad_mag, grad_down)


def solution(mesh):
    placed = (
        P(("groups", "dp"), "tensor"),
        P(("groups", "dp"), None),
        P(("groups", "dp"), None),
        P(("groups", "dp")),
        P("dp", "tensor"),
        P(None, None, "tensor"),
        P(None, "dp", None),
        P(None, "dp"),
    )
    return jax.shard_map(
        local,
        mesh=mesh,
        in_specs=placed,
        out_specs=(
            P("groups", ("dp", "tensor"), None),
            P("groups", ("dp", "tensor")),
            P(("groups", "dp"), "tensor"),
        ),
        check_vma=False,
    )
```

```python
import functools

import jax
import jax.numpy as jnp
from jax import lax
from jax.experimental import pallas as pl
from jax.experimental.pallas import tpu as pltpu
from jax.sharding import PartitionSpec as P


def plain(
    inputs,
    output_gradient,
    frozen_output,
    tenant_of_tile,
    frozen_weight,
    adapter_down,
    adapter_up,
    magnitude,
):
    hi = lax.Precision.HIGHEST
    tenant_list, rank_dimension, input_local = adapter_down.shape
    own_rows = frozen_weight.shape[0]
    token_rows = inputs.shape[0]
    tile_count = tenant_of_tile.shape[0]
    tile_len = token_rows // tile_count
    tensor_count = lax.axis_size("tensor")
    data_count = lax.axis_size("dp")
    row_halves_split = own_rows // tensor_count
    span_cols = data_count * row_halves_split
    shifted_values = jnp.einsum(
        "sxh,shj->sxj", adapter_up, adapter_down, preferred_element_type=jnp.float32
    )
    merged = frozen_weight.astype(jnp.float32)[None] + shifted_values
    partial_sq = jnp.sum(merged * merged, axis=2)
    tile_onehot = (
        tenant_of_tile[:, None] == jnp.arange(tenant_list, dtype=jnp.int32)[None, :]
    ).astype(jnp.float32)
    row_tenant = jnp.repeat(jnp.arange(tenant_list, dtype=jnp.int32), rank_dimension)
    row_rank = jnp.tile(jnp.arange(rank_dimension, dtype=jnp.int32), tenant_list)
    col_tenant = jnp.repeat(tenant_of_tile, rank_dimension)
    col_rank = jnp.tile(jnp.arange(rank_dimension, dtype=jnp.int32), tile_count)
    placement = (
        (row_tenant[:, None] == col_tenant[None, :]) & (row_rank[:, None] == col_rank[None, :])
    ).astype(jnp.float32)
    tile_inputs = inputs.reshape(tile_count, tile_len, input_local)
    selected_down = jnp.take(adapter_down, tenant_of_tile, axis=0)
    rank_part = jnp.einsum(
        "tsi,tri->tsr", tile_inputs, selected_down, preferred_element_type=jnp.float32
    )
    norm_sq = lax.psum(partial_sq, "tensor")
    rank_sum = lax.psum(rank_part, "tensor")
    norm_values = jnp.sqrt(norm_sq)
    tile_position = lax.axis_index("tensor") * row_halves_split
    scale_own = lax.dynamic_slice_in_dim(
        magnitude / norm_values, tile_position, row_halves_split, 1
    )
    norm_own = lax.dynamic_slice_in_dim(norm_values, tile_position, row_halves_split, 1)
    owned_up_rows = lax.dynamic_slice_in_dim(adapter_up, tile_position, row_halves_split, 1)
    scales = lax.all_gather(scale_own, "dp", axis=1, tiled=True)
    up_cols = lax.all_gather(owned_up_rows, "dp", axis=1, tiled=True)

    def select_cols(full):
        shaped = full.reshape(token_rows, data_count, tensor_count, row_halves_split)
        picked = lax.dynamic_index_in_dim(shaped, lax.axis_index("tensor"), 2, keepdims=False)
        return picked.reshape(tile_count, tile_len, span_cols)

    grad_cols = select_cols(output_gradient)
    base_cols = select_cols(frozen_output)
    rank_low = rank_sum.astype(jnp.bfloat16)
    up_sel = jnp.take(up_cols, tenant_of_tile, axis=0)
    scale_sel = jnp.take(scales, tenant_of_tile, axis=0)
    mixed_out = base_cols.astype(jnp.float32) + jnp.einsum(
        "tsr,tor->tso", rank_low, up_sel, preferred_element_type=jnp.float32
    )
    grad_f = grad_cols.astype(jnp.float32)
    tile_mag = jnp.sum(grad_f * mixed_out, axis=1)
    mag_part = jnp.dot(tile_onehot.T, tile_mag, precision=hi)
    scaled_grad = (grad_f * scale_sel[:, None, :]).astype(jnp.bfloat16)
    up_tile = jnp.einsum("tsr,tso->tro", rank_low, scaled_grad, preferred_element_type=jnp.float32)
    up_part = jnp.dot(
        placement, up_tile.reshape(tile_count * rank_dimension, span_cols), precision=hi
    )
    back_part = jnp.einsum("tso,tor->tsr", scaled_grad, up_sel, preferred_element_type=jnp.float32)
    back_sum = lax.psum(back_part, "tensor")
    back_low = back_sum.astype(jnp.bfloat16)
    down_tile = jnp.einsum(
        "tsr,tsi->tri", back_low, tile_inputs, preferred_element_type=jnp.float32
    ).reshape(tile_count * rank_dimension, input_local)
    up_sum = lax.psum_scatter(up_part, "dp", scatter_dimension=1, tiled=True)
    mag_sum = lax.psum_scatter(mag_part, "dp", scatter_dimension=1, tiled=True)
    grad_mag = mag_sum / norm_own
    grad_up = jnp.transpose(
        up_sum.reshape(tenant_list, rank_dimension, row_halves_split), (0, 2, 1)
    )
    down_part = jnp.dot(placement, down_tile, precision=hi)
    grad_down = lax.psum_scatter(down_part, "dp", scatter_dimension=0, tiled=True)
    return (grad_up, grad_mag, grad_down)


F32 = jnp.float32
CHUNK = 512
BF16 = jnp.bfloat16
NT = (((1,), (1,)), ((), ()))


def iota(shape, dim):
    return lax.broadcasted_iota(jnp.int32, shape, dim)


def exchange_kernel(
    N, T, K, R,
    ten_ref, x_hbm, g_hbm, f_hbm, down_hbm, w_hbm, up_ref, mag_ref,
    up_out, mag_out, down_out,
    x_ref, g_ref, f_ref, down_ref, w_ref, um, sq_acc, sq_send,
    g_buf, aux_send, aux_buf, sq_buf, rp_send, rp_buf, ra_buf, up_acc, z_acc, fg_acc,
    back_send, back_buf, tile_send, tile_buf, part_send, part_buf,
    load, g_ss, g_rs, aux_ss, aux_rs, pair_ss, pair_rs, ra_ss, ra_rs, sq_rs,
    back_ss, back_rs, tile_ss, tile_rs, part_ss, part_rs,
):
    me = lax.axis_index("dp")
    core = lax.axis_index("tensor")
    other = 1 - core
    tok = x_ref.shape[0]
    half = tok // 2
    width = x_ref.shape[1] // N
    C = mag_ref.shape[1] // T
    KR = K * R
    group = lax.axis_index("groups")

    loads = [
        pltpu.make_async_copy(down_hbm, down_ref, load.at[0]),
        pltpu.make_async_copy(x_hbm, x_ref, load.at[1]),
        pltpu.make_async_copy(
            w_hbm.at[pl.ds(pl.multiple_of(group * C, C), C), :], w_ref, load.at[2]
        ),
        pltpu.make_async_copy(g_hbm, g_ref, load.at[3]),
        pltpu.make_async_copy(f_hbm, f_ref, load.at[4]),
    ]
    for one in loads:
        one.start()

    def copy(src, dst, ss, rs, dp, tensor):
        return pltpu.make_async_remote_copy(
            src_ref=src, dst_ref=dst, send_sem=ss, recv_sem=rs,
            device_id={"dp": dp, "tensor": tensor}, device_id_type=pl.DeviceIdType.MESH,
        )

    def peer(off):
        return lax.rem(me + off, N)

    barrier = pltpu.get_barrier_semaphore()
    for off in range(N):
        for t in ((other,) if off == 0 else (core, other)):
            pl.semaphore_signal(
                barrier, inc=1, device_id={"dp": peer(off), "tensor": t},
                device_id_type=pl.DeviceIdType.MESH,
            )
    for t in range(T):
        pl.semaphore_signal(
            barrier, inc=1, device_id={"groups": 1 - group, "dp": me, "tensor": t},
            device_id_type=pl.DeviceIdType.MESH,
        )
    pl.semaphore_wait(barrier, 2 * N - 1 + T)

    def cols(d):
        return pl.ds(pl.multiple_of((d * T + core) * C, C), C)

    def span(d):
        return pl.ds(pl.multiple_of(d * width, width), width)

    def g_copy(d):
        return copy(g_hbm.at[:, cols(d)], g_buf.at[me], g_ss.at[d], g_rs.at[me], d, core)

    def aux_copy(d):
        return copy(aux_send.at[d], aux_buf.at[me], aux_ss.at[d], aux_rs.at[me], d, core)

    def start_g(off, _):
        g_copy(peer(off)).start()
        return 0
    lax.fori_loop(1, N, start_g, 0)

    ten0 = ten_ref[0]
    ten1 = ten_ref[1]
    lane_tok = iota((1, tok), 1)
    own_ten = jnp.where(lane_tok < half, ten0, ten1)
    own_mask = (iota((KR, tok), 0) // R) == own_ten

    loads[0].wait()
    loads[1].wait()
    proj = lax.dot_general(down_ref[...], x_ref[...], NT, preferred_element_type=F32)
    rp_send[...] = jnp.sum(jnp.where(own_mask, proj, 0.0).reshape(K, R, tok), axis=0)
    rp_copy = copy(rp_send, rp_buf, pair_ss.at[1], pair_rs.at[1], me, other)
    rp_copy.start()

    lane = iota((1, C), 1)
    rows = iota((8, C), 0)
    ids0 = jnp.full((1, C), ten0, jnp.int32)
    ids1 = jnp.full((1, C), ten1, jnp.int32)
    tok_ids = jnp.where(lax.rem(lane, tok) < half, ten0, ten1)
    slot_ids = jnp.where(lane // (2 * R) == me, jnp.where(lax.rem(lane, 2 * R) < R, ten0, ten1), 0)
    ids = jnp.where(rows == 2, ids0, jnp.where(rows == 3, ids1, jnp.where(rows == 4, tok_ids, slot_ids)))
    ids = jnp.where((rows >= 2) & (rows <= 5), ids, 0).astype(F32)

    loads[3].wait()
    loads[4].wait()

    def make_aux(off, _):
        d = peer(off)
        prod = g_ref[:, cols(d)].astype(F32) * f_ref[:, cols(d)].astype(F32)
        s0 = jnp.sum(prod[:half], axis=0, keepdims=True)
        s1 = jnp.sum(prod[half:], axis=0, keepdims=True)
        aux_send[d] = jnp.where(rows == 0, s0, jnp.where(rows == 1, s1, ids))
        return 0

    def start_aux(off, _):
        make_aux(off, 0)
        aux_copy(peer(off)).start()
        return 0
    lax.fori_loop(1, N, start_aux, 0)
    make_aux(0, 0)
    aux_buf[me] = aux_send[me]
    g_buf[me] = g_ref[:, cols(me)]

    rp_copy.wait_recv()
    a = rp_send[...]
    b = rp_buf[...]
    ra_buf[me] = (a + b).astype(BF16)

    def ra_copy(d):
        return copy(ra_buf.at[me], ra_buf.at[me], ra_ss.at[d], ra_rs.at[me], d, core)

    def start_ra(off, _):
        ra_copy(peer(off)).start()
        return 0
    lax.fori_loop(1, N, start_ra, 0)

    loads[2].wait()
    ut = up_ref[:, pl.ds(pl.multiple_of(group * C, C), C)].astype(F32).T
    for k in range(K):
        um[k] = jnp.where(iota((C, KR), 1) // R == k, ut, 0.0).astype(BF16)
    sq_acc[...] = jnp.zeros_like(sq_acc)

    def norm_chunk(c, _):
        at = pl.ds(pl.multiple_of(c * CHUNK, CHUNK), CHUNK)
        w = w_ref[:, at].astype(F32)
        d = down_ref[:, at]
        for k in range(K):
            m = w + jnp.dot(um[k], d, preferred_element_type=F32)
            m = m * m
            total = m[:, :128]
            for b in range(128, CHUNK, 128):
                total = total + m[:, b:b + 128]
            sq_acc[k] += total
        return 0
    lax.fori_loop(0, w_ref.shape[1] // CHUNK, norm_chunk, 0)
    square = jnp.zeros((C, 128), F32)
    for k in range(K):
        square = jnp.where(iota((C, 128), 1) == k, jnp.sum(sq_acc[k], axis=1, keepdims=True), square)
    sq_send[...] = square.T[:K]

    def sq_copy(gr, i):
        return pltpu.make_async_remote_copy(
            src_ref=sq_send, dst_ref=sq_buf.at[core], send_sem=pair_ss.at[i],
            recv_sem=sq_rs.at[core], device_id={"groups": gr, "dp": me, "tensor": group},
            device_id_type=pl.DeviceIdType.MESH,
        )
    sq_copy(1 - group, 0).start()

    @pl.when(core == group)
    def _():
        sq_buf[core] = sq_send[...]

    @pl.when(core != group)
    def _():
        sq_copy(group, 2).start()

    def wait_sq(t):
        copy(sq_send, sq_buf.at[t], pair_ss.at[0], sq_rs.at[t], me, other).wait_recv()
    wait_sq(other)

    @pl.when(core != group)
    def _():
        wait_sq(core)
        sq_copy(group, 2).wait_send()
    sq_copy(1 - group, 0).wait_send()
    own = pl.ds(pl.multiple_of(core * C, C), C)
    norm = jnp.sqrt(sq_buf[0] + sq_buf[1])
    scale = mag_ref[:, own] / norm
    up = up_ref[:, own]

    up_acc[...] = jnp.zeros_like(up_acc)
    z_acc[...] = jnp.zeros_like(z_acc)
    fg_acc[...] = jnp.zeros_like(fg_acc)

    def owner_block(s):
        aux = aux_buf[s]
        fg = fg_acc[...]
        sel0 = jnp.zeros((1, C), F32)
        sel1 = jnp.zeros((1, C), F32)
        krow = iota((K, C), 0).astype(F32)
        hit0 = krow == aux[2:3]
        hit1 = krow == aux[3:4]
        fg_acc[...] = fg + jnp.where(hit0, aux[0:1], 0.0) + jnp.where(hit1, aux[1:2], 0.0)
        sel0 = jnp.sum(jnp.where(hit0, scale, 0.0), axis=0, keepdims=True)
        sel1 = jnp.sum(jnp.where(hit1, scale, 0.0), axis=0, keepdims=True)
        g = g_buf[s]
        gf = g.astype(F32)
        scaled = (gf * jnp.where(iota((tok, C), 0) < half, sel0, sel1)).astype(BF16)
        mask = (iota((KR, tok), 0) // R).astype(F32) == aux[4:5, :tok]
        ra = ra_buf[s].astype(F32)
        wide = jnp.where(mask, jnp.concatenate([ra] * K, axis=0), 0.0).astype(BF16)
        up_acc[...] += jnp.dot(wide, scaled, preferred_element_type=F32)
        z_acc[...] += jnp.dot(wide, g, preferred_element_type=F32)
        back = lax.dot_general(up, scaled, NT, preferred_element_type=F32)
        return jnp.sum(jnp.where(mask, back, 0.0).reshape(K, R, tok), axis=0)

    mine = me * T + core

    def back_copy(s, t):
        return copy(
            back_send.at[s], back_buf.at[mine], back_ss.at[s * T + t], back_rs.at[mine], s, t
        )

    own_back = owner_block(me)
    back_send[me] = own_back
    back_copy(me, other).start()
    back_buf[mine] = own_back

    def remote_block(off, _):
        s = peer(off)
        copy(aux_send.at[s], aux_buf.at[s], aux_ss.at[s], aux_rs.at[s], s, core).wait_recv()
        copy(ra_buf.at[s], ra_buf.at[s], ra_ss.at[s], ra_rs.at[s], s, core).wait_recv()
        copy(g_buf.at[s], g_buf.at[s], g_ss.at[s], g_rs.at[s], s, core).wait_recv()
        back_send[s] = owner_block(s)
        back_copy(s, core).start()
        back_copy(s, other).start()
        return 0
    lax.fori_loop(1, N, remote_block, 0)

    up_sum = up_acc[...]
    up_out[...] = up_sum
    mixed = jnp.sum((up.astype(F32) * z_acc[...]).reshape(K, R, C), axis=1)
    mag_out[...] = (fg_acc[...] + mixed) / norm

    def wait_back(s, t):
        i = s * T + t
        copy(back_send.at[s], back_buf.at[i], back_ss.at[i], back_rs.at[i], s, t).wait_recv()

    def wait_backs(off, _):
        wait_back(peer(off), core)
        wait_back(peer(off), other)
        return 0
    wait_back(me, other)
    lax.fori_loop(1, N, wait_backs, 0)
    rank_grad = jnp.sum(back_buf[...], axis=0).astype(BF16).astype(F32)
    two = jnp.concatenate([rank_grad, rank_grad], axis=0)
    lhs = jnp.where((iota((2 * R, tok), 0) // R) == (iota((2 * R, tok), 1) // half), two, 0.0).astype(BF16)

    def tile_copy(d):
        return copy(tile_send.at[d], tile_buf.at[me], tile_ss.at[d], tile_rs.at[me], d, core)

    def start_tile(off, _):
        d = peer(off)
        tile_send[d] = jnp.dot(lhs, x_ref[:, span(d)], preferred_element_type=F32).astype(BF16)
        tile_copy(d).start()
        return 0
    lax.fori_loop(1, N, start_tile, 0)
    tile_buf[me] = jnp.dot(lhs, x_ref[:, span(me)], preferred_element_type=F32).astype(BF16)

    slot_ten = jnp.sum(aux_buf[:, 5, :], axis=0, keepdims=True)
    prow = iota((KR, C), 0)
    place = ((prow // R).astype(F32) == slot_ten) & (lax.rem(prow, R) == lax.rem(iota((KR, C), 1), R))
    place = jnp.where(place, 1.0, 0.0).astype(BF16)

    def wait_tile(off, _):
        s = peer(off)
        copy(tile_send.at[s], tile_buf.at[s], tile_ss.at[s], tile_rs.at[s], s, core).wait_recv()
        return 0
    lax.fori_loop(1, N, wait_tile, 0)
    part = jnp.dot(place, tile_buf[...].reshape(N * 2 * R, width), preferred_element_type=F32)
    part_send[...] = part.astype(BF16).reshape(N, R, width)

    def part_copy(d):
        return copy(part_send.at[d], part_buf.at[me], part_ss.at[d], part_rs.at[me], d, core)

    def start_part(off, _):
        part_copy(peer(off)).start()
        return 0
    lax.fori_loop(1, N, start_part, 0)
    part_buf[me] = part_send[me]

    def wait_sends(off, _):
        d = peer(off)
        g_copy(d).wait_send()
        aux_copy(d).wait_send()
        ra_copy(d).wait_send()
        back_copy(d, core).wait_send()
        back_copy(d, other).wait_send()
        tile_copy(d).wait_send()
        return 0
    rp_copy.wait_send()
    back_copy(me, other).wait_send()
    lax.fori_loop(1, N, wait_sends, 0)

    down_out[:, span(me)] = part_buf[me].astype(F32)

    def finish(off, _):
        s = peer(off)
        copy(part_send.at[s], part_buf.at[s], part_ss.at[s], part_rs.at[s], s, core).wait_recv()
        down_out[:, span(s)] = part_buf[s].astype(F32)
        part_copy(s).wait_send()
        return 0
    lax.fori_loop(1, N, finish, 0)


def exchange(ten, x, g, f, down, w, up, mag, N, T, K, R):
    tok, I = x.shape
    O = g.shape[1]
    C = up.shape[1] // T
    width = I // N
    vm = pltpu.VMEM
    dma = pltpu.SemaphoreType.DMA
    spec = pl.BlockSpec(memory_space=pltpu.VMEM)
    hbm = pl.BlockSpec(memory_space=pl.ANY)
    return pl.pallas_call(
        functools.partial(exchange_kernel, N, T, K, R),
        out_shape=(
            jax.ShapeDtypeStruct((K * R, C), F32),
            jax.ShapeDtypeStruct((K, C), F32),
            jax.ShapeDtypeStruct((R, I), F32),
        ),
        in_specs=[pl.BlockSpec(memory_space=pltpu.SMEM)] + [hbm] * 5 + [spec] * 2,
        out_specs=(spec, spec, spec),
        scratch_shapes=[
            vm((tok, I), BF16), vm((tok, O), BF16), vm((tok, O), BF16), vm((K * R, I), BF16),
            vm((C, I), BF16), vm((K, C, K * R), BF16), vm((K, C, 128), F32), vm((K, C), F32),
            vm((N, tok, C), BF16), vm((N, 8, C), F32), vm((N, 8, C), F32), vm((T, K, C), F32),
            vm((R, tok), F32), vm((R, tok), F32), vm((N, R, tok), BF16),
            vm((K * R, C), F32), vm((K * R, C), F32), vm((K, C), F32),
            vm((N, R, tok), F32), vm((N * T, R, tok), F32),
            vm((N, 2 * R, width), BF16), vm((N, 2 * R, width), BF16),
            vm((N, R, width), BF16), vm((N, R, width), BF16),
            dma((5,)),
            dma((N,)), dma((N,)), dma((N,)), dma((N,)), dma((3,)), dma((3,)),
            dma((N,)), dma((N,)), dma((T,)), dma((N * T,)), dma((N * T,)),
            dma((N,)), dma((N,)), dma((N,)), dma((N,)),
        ],
        compiler_params=pltpu.CompilerParams(
            collective_id=0, has_side_effects=True, vmem_limit_bytes=56 * 1024 * 1024
        ),
    )(ten, x, g, f, down, w, up, mag)


def local(
    inputs,
    output_gradient,
    frozen_output,
    tenant_of_tile,
    frozen_weight,
    adapter_down,
    adapter_up,
    magnitude,
):
    K, R, I = adapter_down.shape
    N = lax.axis_size("dp")
    T = lax.axis_size("tensor")
    own = frozen_weight.shape[0]
    C = own // T
    if not (
        N == K and T == 2 and lax.axis_size("groups") == 2 and R == 16 and K == 8 and C == N * 2 * R
        and inputs.shape[0] == 128 and tenant_of_tile.shape[0] == 2 and I % CHUNK == 0 and I % (128 * N) == 0
    ):
        return plain(
            inputs, output_gradient, frozen_output, tenant_of_tile,
            frozen_weight, adapter_down, adapter_up, magnitude,
        )
    up = jnp.transpose(adapter_up, (0, 2, 1)).reshape(K * R, own)
    up_sum, grad_mag, grad_down = exchange(
        tenant_of_tile, inputs, output_gradient, frozen_output,
        adapter_down.reshape(K * R, I), frozen_weight, up, magnitude, N, T, K, R,
    )
    grad_up = jnp.transpose(up_sum.reshape(K, R, C), (0, 2, 1))
    return (grad_up, grad_mag, grad_down)


def solution(mesh):
    placed = (
        P(("groups", "dp"), "tensor"),
        P(("groups", "dp"), None),
        P(("groups", "dp"), None),
        P(("groups", "dp")),
        P("dp", "tensor"),
        P(None, None, "tensor"),
        P(None, "dp", None),
        P(None, "dp"),
    )
    return jax.shard_map(
        local,
        mesh=mesh,
        in_specs=placed,
        out_specs=(
            P("groups", ("dp", "tensor"), None),
            P("groups", ("dp", "tensor")),
            P(("groups", "dp"), "tensor"),
        ),
        check_vma=False,
    )
```

```python
import functools

import jax
import jax.numpy as jnp
from jax import lax
from jax.experimental import pallas as pl
from jax.experimental.pallas import tpu as pltpu
from jax.sharding import PartitionSpec as P


def plain(
    inputs,
    output_gradient,
    frozen_output,
    tenant_of_tile,
    frozen_weight,
    adapter_down,
    adapter_up,
    magnitude,
):
    hi = lax.Precision.HIGHEST
    tenant_list, rank_dimension, input_local = adapter_down.shape
    own_rows = frozen_weight.shape[0]
    token_rows = inputs.shape[0]
    tile_count = tenant_of_tile.shape[0]
    tile_len = token_rows // tile_count
    tensor_count = lax.axis_size("tensor")
    data_count = lax.axis_size("dp")
    row_halves_split = own_rows // tensor_count
    span_cols = data_count * row_halves_split
    shifted_values = jnp.einsum(
        "sxh,shj->sxj", adapter_up, adapter_down, preferred_element_type=jnp.float32
    )
    merged = frozen_weight.astype(jnp.float32)[None] + shifted_values
    partial_sq = jnp.sum(merged * merged, axis=2)
    tile_onehot = (
        tenant_of_tile[:, None] == jnp.arange(tenant_list, dtype=jnp.int32)[None, :]
    ).astype(jnp.float32)
    row_tenant = jnp.repeat(jnp.arange(tenant_list, dtype=jnp.int32), rank_dimension)
    row_rank = jnp.tile(jnp.arange(rank_dimension, dtype=jnp.int32), tenant_list)
    col_tenant = jnp.repeat(tenant_of_tile, rank_dimension)
    col_rank = jnp.tile(jnp.arange(rank_dimension, dtype=jnp.int32), tile_count)
    placement = (
        (row_tenant[:, None] == col_tenant[None, :]) & (row_rank[:, None] == col_rank[None, :])
    ).astype(jnp.float32)
    tile_inputs = inputs.reshape(tile_count, tile_len, input_local)
    selected_down = jnp.take(adapter_down, tenant_of_tile, axis=0)
    rank_part = jnp.einsum(
        "tsi,tri->tsr", tile_inputs, selected_down, preferred_element_type=jnp.float32
    )
    norm_sq = lax.psum(partial_sq, "tensor")
    rank_sum = lax.psum(rank_part, "tensor")
    norm_values = jnp.sqrt(norm_sq)
    tile_position = lax.axis_index("tensor") * row_halves_split
    scale_own = lax.dynamic_slice_in_dim(
        magnitude / norm_values, tile_position, row_halves_split, 1
    )
    norm_own = lax.dynamic_slice_in_dim(norm_values, tile_position, row_halves_split, 1)
    owned_up_rows = lax.dynamic_slice_in_dim(adapter_up, tile_position, row_halves_split, 1)
    scales = lax.all_gather(scale_own, "dp", axis=1, tiled=True)
    up_cols = lax.all_gather(owned_up_rows, "dp", axis=1, tiled=True)

    def select_cols(full):
        shaped = full.reshape(token_rows, data_count, tensor_count, row_halves_split)
        picked = lax.dynamic_index_in_dim(shaped, lax.axis_index("tensor"), 2, keepdims=False)
        return picked.reshape(tile_count, tile_len, span_cols)

    grad_cols = select_cols(output_gradient)
    base_cols = select_cols(frozen_output)
    rank_low = rank_sum.astype(jnp.bfloat16)
    up_sel = jnp.take(up_cols, tenant_of_tile, axis=0)
    scale_sel = jnp.take(scales, tenant_of_tile, axis=0)
    mixed_out = base_cols.astype(jnp.float32) + jnp.einsum(
        "tsr,tor->tso", rank_low, up_sel, preferred_element_type=jnp.float32
    )
    grad_f = grad_cols.astype(jnp.float32)
    tile_mag = jnp.sum(grad_f * mixed_out, axis=1)
    mag_part = jnp.dot(tile_onehot.T, tile_mag, precision=hi)
    scaled_grad = (grad_f * scale_sel[:, None, :]).astype(jnp.bfloat16)
    up_tile = jnp.einsum("tsr,tso->tro", rank_low, scaled_grad, preferred_element_type=jnp.float32)
    up_part = jnp.dot(
        placement, up_tile.reshape(tile_count * rank_dimension, span_cols), precision=hi
    )
    back_part = jnp.einsum("tso,tor->tsr", scaled_grad, up_sel, preferred_element_type=jnp.float32)
    back_sum = lax.psum(back_part, "tensor")
    back_low = back_sum.astype(jnp.bfloat16)
    down_tile = jnp.einsum(
        "tsr,tsi->tri", back_low, tile_inputs, preferred_element_type=jnp.float32
    ).reshape(tile_count * rank_dimension, input_local)
    up_sum = lax.psum_scatter(up_part, "dp", scatter_dimension=1, tiled=True)
    mag_sum = lax.psum_scatter(mag_part, "dp", scatter_dimension=1, tiled=True)
    grad_mag = mag_sum / norm_own
    grad_up = jnp.transpose(
        up_sum.reshape(tenant_list, rank_dimension, row_halves_split), (0, 2, 1)
    )
    down_part = jnp.dot(placement, down_tile, precision=hi)
    grad_down = lax.psum_scatter(down_part, "dp", scatter_dimension=0, tiled=True)
    return (grad_up, grad_mag, grad_down)


F32 = jnp.float32
CHUNK = 512
BF16 = jnp.bfloat16
NT = (((1,), (1,)), ((), ()))


def iota(shape, dim):
    return lax.broadcasted_iota(jnp.int32, shape, dim)


def exchange_kernel(
    N, T, K, R,
    ten_ref, x_hbm, g_hbm, f_hbm, down_hbm, w_hbm, up_ref, mag_ref,
    up_out, mag_out, down_out,
    x_ref, g_ref, f_ref, down_ref, w_ref, um, sq_acc, sq_send,
    g_buf, aux_send, aux_buf, sq_buf, rp_send, rp_buf, ra_buf, up_acc, z_acc, fg_acc,
    back_send, back_buf, tile_send, tile_buf, part_send, part_buf,
    load, g_ss, g_rs, aux_ss, aux_rs, pair_ss, pair_rs, ra_ss, ra_rs, sq_rs,
    back_ss, back_rs, tile_ss, tile_rs, part_ss, part_rs,
):
    me = lax.axis_index("dp")
    core = lax.axis_index("tensor")
    other = 1 - core
    tok = x_ref.shape[0]
    half = tok // 2
    width = x_ref.shape[1] // N
    C = mag_ref.shape[1] // T
    KR = K * R
    group = lax.axis_index("groups")

    loads = [
        pltpu.make_async_copy(down_hbm, down_ref, load.at[0]),
        pltpu.make_async_copy(x_hbm, x_ref, load.at[1]),
        pltpu.make_async_copy(
            w_hbm.at[pl.ds(pl.multiple_of(group * C, C), C), :], w_ref, load.at[2]
        ),
        pltpu.make_async_copy(g_hbm, g_ref, load.at[3]),
        pltpu.make_async_copy(f_hbm, f_ref, load.at[4]),
    ]
    for one in loads:
        one.start()

    def copy(src, dst, ss, rs, dp, tensor):
        return pltpu.make_async_remote_copy(
            src_ref=src, dst_ref=dst, send_sem=ss, recv_sem=rs,
            device_id={"dp": dp, "tensor": tensor}, device_id_type=pl.DeviceIdType.MESH,
        )

    def peer(off):
        return lax.rem(me + off, N)

    barrier = pltpu.get_barrier_semaphore()
    for off in range(N):
        for t in ((other,) if off == 0 else (core, other)):
            pl.semaphore_signal(
                barrier, inc=1, device_id={"dp": peer(off), "tensor": t},
                device_id_type=pl.DeviceIdType.MESH,
            )
    for t in range(T):
        pl.semaphore_signal(
            barrier, inc=1, device_id={"groups": 1 - group, "dp": me, "tensor": t},
            device_id_type=pl.DeviceIdType.MESH,
        )
    pl.semaphore_wait(barrier, 2 * N - 1 + T)

    def cols(d):
        return pl.ds(pl.multiple_of((d * T + core) * C, C), C)

    def span(d):
        return pl.ds(pl.multiple_of(d * width, width), width)

    def g_copy(d):
        return copy(g_hbm.at[:, cols(d)], g_buf.at[me], g_ss.at[d], g_rs.at[me], d, core)

    def aux_copy(d):
        return copy(aux_send.at[d], aux_buf.at[me], aux_ss.at[d], aux_rs.at[me], d, core)

    def start_g(off, _):
        g_copy(peer(off)).start()
        return 0
    lax.fori_loop(1, N, start_g, 0)

    ten0 = ten_ref[0]
    ten1 = ten_ref[1]
    lane_tok = iota((1, tok), 1)
    own_ten = jnp.where(lane_tok < half, ten0, ten1)
    own_mask = (iota((KR, tok), 0) // R) == own_ten

    loads[0].wait()
    loads[1].wait()
    proj = lax.dot_general(down_ref[...], x_ref[...], NT, preferred_element_type=F32)
    rp_send[...] = jnp.sum(jnp.where(own_mask, proj, 0.0).reshape(K, R, tok), axis=0)
    rp_copy = copy(rp_send, rp_buf, pair_ss.at[1], pair_rs.at[1], me, other)
    rp_copy.start()

    lane = iota((1, C), 1)
    rows = iota((8, C), 0)
    ids0 = jnp.full((1, C), ten0, jnp.int32)
    ids1 = jnp.full((1, C), ten1, jnp.int32)
    tok_ids = jnp.where(lax.rem(lane, tok) < half, ten0, ten1)
    slot_ids = jnp.where(lane // (2 * R) == me, jnp.where(lax.rem(lane, 2 * R) < R, ten0, ten1), 0)
    ids = jnp.where(rows == 2, ids0, jnp.where(rows == 3, ids1, jnp.where(rows == 4, tok_ids, slot_ids)))
    ids = jnp.where((rows >= 2) & (rows <= 5), ids, 0).astype(F32)

    loads[3].wait()
    loads[4].wait()

    def make_aux(off, _):
        d = peer(off)
        prod = g_ref[:, cols(d)].astype(F32) * f_ref[:, cols(d)].astype(F32)
        s0 = jnp.sum(prod[:half], axis=0, keepdims=True)
        s1 = jnp.sum(prod[half:], axis=0, keepdims=True)
        aux_send[d] = jnp.where(rows == 0, s0, jnp.where(rows == 1, s1, ids))
        return 0

    def start_aux(off, _):
        make_aux(off, 0)
        aux_copy(peer(off)).start()
        return 0
    lax.fori_loop(1, N, start_aux, 0)
    make_aux(0, 0)
    aux_buf[me] = aux_send[me]
    g_buf[me] = g_ref[:, cols(me)]

    rp_copy.wait_recv()
    a = rp_send[...]
    b = rp_buf[...]
    ra_buf[me] = (a + b).astype(BF16)

    def ra_copy(d):
        return copy(ra_buf.at[me], ra_buf.at[me], ra_ss.at[d], ra_rs.at[me], d, core)

    def start_ra(off, _):
        ra_copy(peer(off)).start()
        return 0
    lax.fori_loop(1, N, start_ra, 0)

    loads[2].wait()
    ut = up_ref[:, pl.ds(pl.multiple_of(group * C, C), C)].astype(F32).T
    for k in range(K):
        um[k] = jnp.where(iota((C, KR), 1) // R == k, ut, 0.0).astype(BF16)
    sq_acc[...] = jnp.zeros_like(sq_acc)

    def norm_chunk(c, _):
        at = pl.ds(pl.multiple_of(c * CHUNK, CHUNK), CHUNK)
        w = w_ref[:, at].astype(F32)
        d = down_ref[:, at]
        for k in range(K):
            m = w + jnp.dot(um[k], d, preferred_element_type=F32)
            m = m * m
            total = m[:, :128]
            for b in range(128, CHUNK, 128):
                total = total + m[:, b:b + 128]
            sq_acc[k] += total
        return 0
    lax.fori_loop(0, w_ref.shape[1] // CHUNK, norm_chunk, 0)
    square = jnp.zeros((C, 128), F32)
    for k in range(K):
        square = jnp.where(iota((C, 128), 1) == k, jnp.sum(sq_acc[k], axis=1, keepdims=True), square)
    sq_send[...] = square.T[:K]

    def sq_copy(gr, i):
        return pltpu.make_async_remote_copy(
            src_ref=sq_send, dst_ref=sq_buf.at[core], send_sem=pair_ss.at[i],
            recv_sem=sq_rs.at[core], device_id={"groups": gr, "dp": me, "tensor": group},
            device_id_type=pl.DeviceIdType.MESH,
        )
    sq_copy(1 - group, 0).start()

    @pl.when(core == group)
    def _():
        sq_buf[core] = sq_send[...]

    @pl.when(core != group)
    def _():
        sq_copy(group, 2).start()

    def wait_sq(t):
        copy(sq_send, sq_buf.at[t], pair_ss.at[0], sq_rs.at[t], me, other).wait_recv()
    wait_sq(other)

    @pl.when(core != group)
    def _():
        wait_sq(core)
        sq_copy(group, 2).wait_send()
    sq_copy(1 - group, 0).wait_send()
    own = pl.ds(pl.multiple_of(core * C, C), C)
    norm = jnp.sqrt(sq_buf[0] + sq_buf[1])
    scale = mag_ref[:, own] / norm
    up = up_ref[:, own]

    up_acc[...] = jnp.zeros_like(up_acc)
    z_acc[...] = jnp.zeros_like(z_acc)
    fg_acc[...] = jnp.zeros_like(fg_acc)

    def owner_block(s):
        aux = aux_buf[s]
        fg = fg_acc[...]
        sel0 = jnp.zeros((1, C), F32)
        sel1 = jnp.zeros((1, C), F32)
        krow = iota((K, C), 0).astype(F32)
        hit0 = krow == aux[2:3]
        hit1 = krow == aux[3:4]
        fg_acc[...] = fg + jnp.where(hit0, aux[0:1], 0.0) + jnp.where(hit1, aux[1:2], 0.0)
        sel0 = jnp.sum(jnp.where(hit0, scale, 0.0), axis=0, keepdims=True)
        sel1 = jnp.sum(jnp.where(hit1, scale, 0.0), axis=0, keepdims=True)
        g = g_buf[s]
        gf = g.astype(F32)
        scaled = (gf * jnp.where(iota((tok, C), 0) < half, sel0, sel1)).astype(BF16)
        mask = (iota((KR, tok), 0) // R).astype(F32) == aux[4:5, :tok]
        ra = ra_buf[s].astype(F32)
        wide = jnp.where(mask, jnp.concatenate([ra] * K, axis=0), 0.0).astype(BF16)
        up_acc[...] += jnp.dot(wide, scaled, preferred_element_type=F32)
        z_acc[...] += jnp.dot(wide, g, preferred_element_type=F32)
        back = lax.dot_general(up, scaled, NT, preferred_element_type=F32)
        return jnp.sum(jnp.where(mask, back, 0.0).reshape(K, R, tok), axis=0)

    mine = me * T + core

    def back_copy(s, t):
        return copy(
            back_send.at[s], back_buf.at[mine], back_ss.at[s * T + t], back_rs.at[mine], s, t
        )

    own_back = owner_block(me)
    back_send[me] = own_back
    back_copy(me, other).start()
    back_buf[mine] = own_back

    def remote_block(off, _):
        s = peer(off)
        copy(aux_send.at[s], aux_buf.at[s], aux_ss.at[s], aux_rs.at[s], s, core).wait_recv()
        copy(ra_buf.at[s], ra_buf.at[s], ra_ss.at[s], ra_rs.at[s], s, core).wait_recv()
        copy(g_buf.at[s], g_buf.at[s], g_ss.at[s], g_rs.at[s], s, core).wait_recv()
        back_send[s] = owner_block(s)
        back_copy(s, core).start()
        back_copy(s, other).start()
        return 0
    lax.fori_loop(1, N, remote_block, 0)

    mixed = jnp.sum((up.astype(F32) * z_acc[...]).reshape(K, R, C), axis=1)
    fg_acc[...] = (fg_acc[...] + mixed) / norm
    writes = [
        pltpu.make_async_copy(up_acc, up_out, load.at[0]),
        pltpu.make_async_copy(fg_acc, mag_out, load.at[1]),
    ]
    for one in writes:
        one.start()

    def wait_back(s, t):
        i = s * T + t
        copy(back_send.at[s], back_buf.at[i], back_ss.at[i], back_rs.at[i], s, t).wait_recv()

    def wait_backs(off, _):
        wait_back(peer(off), core)
        wait_back(peer(off), other)
        return 0
    wait_back(me, other)
    lax.fori_loop(1, N, wait_backs, 0)
    rank_grad = jnp.sum(back_buf[...], axis=0).astype(BF16).astype(F32)
    two = jnp.concatenate([rank_grad, rank_grad], axis=0)
    lhs = jnp.where((iota((2 * R, tok), 0) // R) == (iota((2 * R, tok), 1) // half), two, 0.0).astype(BF16)

    def tile_copy(d):
        return copy(tile_send.at[d], tile_buf.at[me], tile_ss.at[d], tile_rs.at[me], d, core)

    def start_tile(off, _):
        d = peer(off)
        tile_send[d] = jnp.dot(lhs, x_ref[:, span(d)], preferred_element_type=F32).astype(BF16)
        tile_copy(d).start()
        return 0
    lax.fori_loop(1, N, start_tile, 0)
    tile_buf[me] = jnp.dot(lhs, x_ref[:, span(me)], preferred_element_type=F32).astype(BF16)

    slot_ten = jnp.sum(aux_buf[:, 5, :], axis=0, keepdims=True)
    prow = iota((KR, C), 0)
    place = ((prow // R).astype(F32) == slot_ten) & (lax.rem(prow, R) == lax.rem(iota((KR, C), 1), R))
    place = jnp.where(place, 1.0, 0.0).astype(BF16)

    def wait_tile(off, _):
        s = peer(off)
        copy(tile_send.at[s], tile_buf.at[s], tile_ss.at[s], tile_rs.at[s], s, core).wait_recv()
        return 0
    lax.fori_loop(1, N, wait_tile, 0)
    part = jnp.dot(place, tile_buf[...].reshape(N * 2 * R, width), preferred_element_type=F32)
    part_send[...] = part.astype(BF16).reshape(N, R, width)

    def part_copy(d):
        return copy(part_send.at[d], part_buf.at[me], part_ss.at[d], part_rs.at[me], d, core)

    def start_part(off, _):
        part_copy(peer(off)).start()
        return 0
    lax.fori_loop(1, N, start_part, 0)
    part_buf[me] = part_send[me]

    def wait_sends(off, _):
        d = peer(off)
        g_copy(d).wait_send()
        aux_copy(d).wait_send()
        ra_copy(d).wait_send()
        back_copy(d, core).wait_send()
        back_copy(d, other).wait_send()
        tile_copy(d).wait_send()
        return 0
    rp_copy.wait_send()
    back_copy(me, other).wait_send()
    lax.fori_loop(1, N, wait_sends, 0)

    down_out[:, span(me)] = part_buf[me].astype(F32)

    def finish(off, _):
        s = peer(off)
        copy(part_send.at[s], part_buf.at[s], part_ss.at[s], part_rs.at[s], s, core).wait_recv()
        down_out[:, span(s)] = part_buf[s].astype(F32)
        part_copy(s).wait_send()
        return 0
    lax.fori_loop(1, N, finish, 0)
    for one in writes:
        one.wait()


def exchange(ten, x, g, f, down, w, up, mag, N, T, K, R):
    tok, I = x.shape
    O = g.shape[1]
    C = up.shape[1] // T
    width = I // N
    vm = pltpu.VMEM
    dma = pltpu.SemaphoreType.DMA
    spec = pl.BlockSpec(memory_space=pltpu.VMEM)
    hbm = pl.BlockSpec(memory_space=pl.ANY)
    return pl.pallas_call(
        functools.partial(exchange_kernel, N, T, K, R),
        out_shape=(
            jax.ShapeDtypeStruct((K * R, C), F32),
            jax.ShapeDtypeStruct((K, C), F32),
            jax.ShapeDtypeStruct((R, I), F32),
        ),
        in_specs=[pl.BlockSpec(memory_space=pltpu.SMEM)] + [hbm] * 5 + [spec] * 2,
        out_specs=(hbm, hbm, spec),
        scratch_shapes=[
            vm((tok, I), BF16), vm((tok, O), BF16), vm((tok, O), BF16), vm((K * R, I), BF16),
            vm((C, I), BF16), vm((K, C, K * R), BF16), vm((K, C, 128), F32), vm((K, C), F32),
            vm((N, tok, C), BF16), vm((N, 8, C), F32), vm((N, 8, C), F32), vm((T, K, C), F32),
            vm((R, tok), F32), vm((R, tok), F32), vm((N, R, tok), BF16),
            vm((K * R, C), F32), vm((K * R, C), F32), vm((K, C), F32),
            vm((N, R, tok), F32), vm((N * T, R, tok), F32),
            vm((N, 2 * R, width), BF16), vm((N, 2 * R, width), BF16),
            vm((N, R, width), BF16), vm((N, R, width), BF16),
            dma((5,)),
            dma((N,)), dma((N,)), dma((N,)), dma((N,)), dma((3,)), dma((3,)),
            dma((N,)), dma((N,)), dma((T,)), dma((N * T,)), dma((N * T,)),
            dma((N,)), dma((N,)), dma((N,)), dma((N,)),
        ],
        compiler_params=pltpu.CompilerParams(
            collective_id=0, has_side_effects=True, vmem_limit_bytes=56 * 1024 * 1024
        ),
    )(ten, x, g, f, down, w, up, mag)


def local(
    inputs,
    output_gradient,
    frozen_output,
    tenant_of_tile,
    frozen_weight,
    adapter_down,
    adapter_up,
    magnitude,
):
    K, R, I = adapter_down.shape
    N = lax.axis_size("dp")
    T = lax.axis_size("tensor")
    own = frozen_weight.shape[0]
    C = own // T
    if not (
        N == K and T == 2 and lax.axis_size("groups") == 2 and R == 16 and K == 8 and C == N * 2 * R
        and inputs.shape[0] == 128 and tenant_of_tile.shape[0] == 2 and I % CHUNK == 0 and I % (128 * N) == 0
    ):
        return plain(
            inputs, output_gradient, frozen_output, tenant_of_tile,
            frozen_weight, adapter_down, adapter_up, magnitude,
        )
    up = jnp.transpose(adapter_up, (0, 2, 1)).reshape(K * R, own)
    up_sum, grad_mag, grad_down = exchange(
        tenant_of_tile, inputs, output_gradient, frozen_output,
        adapter_down.reshape(K * R, I), frozen_weight, up, magnitude, N, T, K, R,
    )
    grad_up = jnp.transpose(up_sum.reshape(K, R, C), (0, 2, 1))
    return (grad_up, grad_mag, grad_down)


def solution(mesh):
    placed = (
        P(("groups", "dp"), "tensor"),
        P(("groups", "dp"), None),
        P(("groups", "dp"), None),
        P(("groups", "dp")),
        P("dp", "tensor"),
        P(None, None, "tensor"),
        P(None, "dp", None),
        P(None, "dp"),
    )
    return jax.shard_map(
        local,
        mesh=mesh,
        in_specs=placed,
        out_specs=(
            P("groups", ("dp", "tensor"), None),
            P("groups", ("dp", "tensor")),
            P(("groups", "dp"), "tensor"),
        ),
        check_vma=False,
    )
```
